128 devices in a mesh: row: 16 (over z, x_lo, core), col: 8 (over y, x_hi).
Axes of the slice: x: 4 (x_hi: 2, x_lo: 2; x = x_hi * 2 + x_lo), y: 4, z: 4, core: 2. Of those that a mesh axis runs over, the one named last changes fastest.
Arguments:
- trials: float32 [2, 512, 1024], P(None, 'col', 'row'), may hold values from -6 to 6
- valence_orb: float32 [512, 8192], P('col', 'row'), may hold values from -0.25 to 0.25
- conduction_orb: float32 [1024, 8192], P('row', 'col'), may hold values from -0.1875 to 0.1875
- screened: float32 [8192, 8192], P('row', 'col'), may hold values from -0.5 to 0.5
Outputs:
- applied: float32 [2, 512, 1024], P(None, 'col', 'row')
The draws below stay inside these ranges and needn't reach their ends.
All inputs are finite; a program needn't handle non-finite values.
Results may differ from the reference program's by a relative error of at most 0.0003.
Values sent between devices are 32-bit elements; how exact they have to be, the bound alone decides.
No kernel may reach another device: no remote copies, remote signals or barrier semaphores. Data moves between devices by JAX's collectives and lax.ppermute only.
A program may use at most 64 MiB of HBM per device.

```python
import jax
import jax.numpy as jnp
from jax import lax

NT = 2
V = 512
C = 1024
POINTS = 8192


def block_levels(own_key, shape, split, least, high):
    def one(position, parts):
        draws = jax.random.uniform(jax.random.fold_in(jax.random.fold_in(own_key, 6), position), (parts,), jnp.float32, least / len(split), high / len(split))
        return jnp.repeat(jnp.exp(draws), shape[position] // parts).reshape((-1,) + (1,) * (len(shape) - position - 1))

    factor_of = one(*split[0])
    for cut in split[1:]:
        factor_of = factor_of * one(*cut)
    return factor_of


def gaussian(own_key, shape, width, reach, cuts=(), held_as=jnp.bfloat16):
    values = jax.random.normal(own_key, shape, jnp.float32) * width
    if len(cuts) > 0:
        values = block_levels(own_key, shape, cuts, -0.22, 0.18) * values
    return jnp.clip(values, min=-reach, max=reach).astype(held_as)


def setup_inputs(seed: int = 0) -> dict:
    arg_keys = jax.random.split(jax.random.key(seed), 5)
    trials = gaussian(arg_keys[0], (NT, V, C), 1.0, 6.0, ((1, 8), (2, 16)), jnp.float32)
    valence_orb = gaussian(arg_keys[1], (V, POINTS), V ** -0.5, 0.25, ((0, 8), (1, 16)), jnp.float32)
    conduction_orb = gaussian(arg_keys[2], (C, POINTS), C ** -0.5, 0.1875, ((0, 16), (1, 8)), jnp.float32)
    screened = gaussian(arg_keys[3], (POINTS, POINTS), (POINTS * POINTS // (V * C)) ** -0.5, 0.5, ((0, 16), (1, 8)), jnp.float32)
    return dict(trials=trials, valence_orb=valence_orb, conduction_orb=conduction_orb, screened=screened)


def reference(trials, valence_orb, conduction_orb, screened):
    highest = lax.Precision.HIGHEST
    block_rows = min(POINTS, 1024)
    block_count = POINTS // block_rows

    def apply_trial(trial_matrix):
        half_encoded = jnp.dot(trial_matrix, conduction_orb, precision=highest, preferred_element_type=jnp.float32)

        def accumulate(total, index):
            offset = (index * block_rows).astype(jnp.int32)
            valence_block = lax.dynamic_slice_in_dim(valence_orb, offset, block_rows, 1)
            screened_block = lax.dynamic_slice_in_dim(screened, offset, block_rows, 0)
            encoded = jnp.dot(valence_block.T, half_encoded, precision=highest, preferred_element_type=jnp.float32)
            pairs = screened_block * encoded
            return total + jnp.dot(valence_block, pairs, precision=highest, preferred_element_type=jnp.float32), None

        total, unused = lax.scan(accumulate, jnp.zeros((V, POINTS), jnp.float32), jnp.arange(block_count, dtype=jnp.int32))
        return jnp.dot(total, conduction_orb.T, precision=highest, preferred_element_type=jnp.float32)

    return lax.map(apply_trial, trials)
```

```python
import jax
import jax.numpy as jnp
from jax import lax
from jax.sharding import Mesh, PartitionSpec as P

AXES = ("z", "xl", "core", "y", "xh")
HIGH = lax.Precision.HIGH


def index(z, x, core, y):
    return (((z * 2 + x % 2) * 2 + core) * 4 + y) * 2 + x // 2


def flip(value, per_core):
    pairs = []
    for z in range(4):
        for x in range(4):
            for core in range(2):
                for y in range(4):
                    if per_core == "core":
                        target = index(z, x, 1 - core, y)
                    else:
                        dz, dx, dy = per_core[core]
                        target = index(z ^ dz, x ^ dx, core, y ^ dy)
                    pairs.append((index(z, x, core, y), target))
    return lax.ppermute(value, AXES, pairs)


Z1, Z3, X1, X2, Y1, Y3 = (1, 0, 0), (3, 0, 0), (0, 1, 0), (0, 2, 0), (0, 0, 1), (0, 0, 3)
ZA, ZB, YA, YB, XL, XH = (Z1, Z3), (Z3, Z1), (Y1, Y3), (Y3, Y1), (X1, X1), (X2, X2)


def grow(value, step, axis):
    return jnp.concatenate([value, flip(value, step)], axis=axis)


def swap_bits(value):
    shape = value.shape
    return value.reshape((2, 2, 2, shape[0] // 8) + shape[1:]).swapaxes(0, 1).reshape(shape)


def halve(value, step, axis):
    size = value.shape[axis] // 2
    kept = lax.slice_in_dim(value, 0, size, axis=axis)
    sent = lax.slice_in_dim(value, size, 2 * size, axis=axis)
    return kept + flip(sent, step)


def dot(spec, a, b):
    return jnp.einsum(spec, a, b, precision=HIGH, preferred_element_type=jnp.float32)


def body(trials, valence, conduction, screened):
    core = lax.axis_index("core")
    mine = lax.dynamic_index_in_dim(trials, core, 0, keepdims=False)
    theirs = lax.dynamic_index_in_dim(trials, 1 - core, 0, keepdims=False)
    trial = jnp.concatenate([mine, flip(theirs, "core")], axis=1)

    c = conduction
    for step in (XL, ZA, ZB):
        c = grow(c, step, 0)
    c_other = swap_bits(flip(c, "core"))
    c_all = jnp.stack([c.reshape(8, 64, -1), c_other.reshape(8, 64, -1)], axis=1).reshape(1024, -1)

    for step in (XL, ZA, ZB):
        trial = grow(trial, step, 1)
    for step in (XH, YA, YB):
        trial = grow(trial, step, 0)

    v = valence
    for step in (XH, YA, YB):
        v = grow(v, step, 0)
    v_other = swap_bits(v)

    half_mine = dot("vc,cn->vn", trial, c_all)
    half_theirs = flip(half_mine, "core")
    pairs_mine = screened * dot("vm,vn->mn", v, half_mine)
    pairs_theirs = screened * dot("vm,vn->mn", v_other, half_theirs)
    sums_theirs = dot("vm,mn->vn", v_other, pairs_theirs)
    sums_mine = dot("vm,mn->vn", v, pairs_mine) + flip(sums_theirs, "core")
    r = dot("vn,cn->vc", sums_mine, c_all)
    for step, axis in ((YB, 0), (ZB, 1), (YA, 0), (ZA, 1), (XH, 0), (XL, 1)):
        r = halve(r, step, axis)
    kept = r[:, :64]
    got = flip(r[:, 64:], "core")
    first = core == 0
    return jnp.stack([jnp.where(first, kept, got), jnp.where(first, got, kept)])


def solution(mesh):
    split = Mesh(mesh.devices.reshape(4, 2, 2, 4, 2), AXES)
    row, col = ("z", "xl", "core"), ("y", "xh")
    placed = (P(None, col, row), P(col, row), P(row, col), P(row, col))
    return jax.shard_map(
        body, mesh=split, in_specs=placed, out_specs=P(None, col, row), check_vma=False
    )
```

```python
import jax
import jax.numpy as jnp
from jax import lax
from jax.sharding import Mesh, PartitionSpec as P

AXES = ("z", "xl", "core", "y", "xh")
HIGH = lax.Precision.HIGH


def index(z, x, core, y):
    return (((z * 2 + x % 2) * 2 + core) * 4 + y) * 2 + x // 2


def flip(value, per_core):
    pairs = []
    for z in range(4):
        for x in range(4):
            for core in range(2):
                for y in range(4):
                    if per_core == "core":
                        target = index(z, x, 1 - core, y)
                    else:
                        dz, dx, dy = per_core[core]
                        target = index(z ^ dz, x ^ dx, core, y ^ dy)
                    pairs.append((index(z, x, core, y), target))
    return lax.ppermute(value, AXES, pairs)


Z1, Z3, X1, X2, Y1, Y3 = (1, 0, 0), (3, 0, 0), (0, 1, 0), (0, 2, 0), (0, 0, 1), (0, 0, 3)
ZA, ZB, YA, YB, XL, XH = (Z1, Z3), (Z3, Z1), (Y1, Y3), (Y3, Y1), (X1, X1), (X2, X2)


def grow(value, step, axis):
    return jnp.concatenate([value, flip(value, step)], axis=axis)


def halves(value, axis):
    size = value.shape[axis] // 2
    return (
        lax.slice_in_dim(value, 0, size, axis=axis),
        lax.slice_in_dim(value, size, 2 * size, axis=axis),
    )


def halve(value, step, axis):
    kept, sent = halves(value, axis)
    return kept + flip(sent, step)


def dot(spec, a, b):
    return jnp.einsum(spec, a, b, precision=HIGH, preferred_element_type=jnp.float32)


def in_parts(v):
    first = v[:, :, :, :32].swapaxes(0, 1).reshape(256, -1)
    return jnp.concatenate([first, v[:, :, :, 32:].reshape(256, -1)], axis=0)


def body(trials, valence, conduction, screened):
    core = lax.axis_index("core")
    mine = lax.dynamic_index_in_dim(trials, core, 0, keepdims=False)
    theirs = lax.dynamic_index_in_dim(trials, 1 - core, 0, keepdims=False)

    c = grow(conduction, XL, 0)
    v = grow(valence, YA, 0)
    t = jnp.concatenate([mine, flip(theirs, "core")], axis=1)
    t = t.reshape(2, 32, 128)
    t = grow(t, ZA, 2)
    t = grow(t, YA, 1)
    t, c, v = lax.optimization_barrier((t, c, v))
    c = grow(c, ZA, 0)
    v = grow(v, XH, 0)
    t = grow(t, XL, 2)
    p, q = t[0], t[1]
    p = grow(p, YB, 0)
    q = grow(q, ZB, 1)
    p, q, c, v = lax.optimization_barrier((p, q, c, v))
    c = grow(c, ZB, 0)
    v = grow(v, YB, 0)
    got = flip(jnp.concatenate([p, q[:, :512], q[:, 512:]], axis=0), XH)
    p = jnp.concatenate([p, got[:128]], axis=0)
    q = jnp.concatenate([q, jnp.concatenate([got[128:192], got[192:]], axis=1)], axis=0)
    p, q, c, v = lax.optimization_barrier((p, q, c, v))
    c_other = flip(c, "core")
    p = grow(p, ZB, 1)
    q = grow(q, YB, 0)
    trial = jnp.concatenate([p, q], axis=0)

    c_own = c.reshape(2, 2, 2, 64, 1024).swapaxes(1, 2)
    c_other = c_other.reshape(2, 2, 2, 64, 1024).transpose(1, 2, 0, 3, 4)
    c_all = jnp.stack([c_own, c_other], axis=3).reshape(1024, 1024)
    v = v.reshape(2, 2, 2, 64, 512)
    v_mine, v_theirs = in_parts(v), in_parts(v.swapaxes(0, 2))

    half_mine = dot("vc,cn->vn", trial, c_all)
    half_theirs = flip(half_mine, "core")
    pairs_mine = screened * dot("vm,vn->mn", v_mine, half_mine)
    pairs_theirs = screened * dot("vm,vn->mn", v_theirs, half_theirs)
    sums_theirs = dot("vm,mn->vn", v_theirs, pairs_theirs)
    sums_mine = dot("vm,mn->vn", v_mine, pairs_mine) + flip(sums_theirs, "core")

    r = dot("vn,cn->vc", sums_mine, c_all)
    p, q = r[:256], r[256:]
    p = halve(p, ZB, 1)
    q = halve(q, YB, 0)
    p = p.reshape(2, 2, 64, 512)
    p = (p[:, 0] + flip(p[:, 1], YB)).reshape(128, 512)
    q = halve(q, ZB, 1)
    r = jnp.stack([p, q]).reshape(4, 2, 32, 512)
    r = (r[:, 0] + flip(r[:, 1], YA)).reshape(128, 512)
    r = r.reshape(128, 2, 2, 128)
    r = (r[:, :, 0] + flip(r[:, :, 1].reshape(128, 256), ZA).reshape(128, 2, 128)).reshape(2, 64, 256)
    r = halve(r, XH, 1).reshape(64, 256)
    r = halve(r, XL, 1)
    kept = r[:, :64]
    got = flip(r[:, 64:], "core")
    first = core == 0
    return jnp.stack([jnp.where(first, kept, got), jnp.where(first, got, kept)])


def solution(mesh):
    split = Mesh(mesh.devices.reshape(4, 2, 2, 4, 2), AXES)
    row, col = ("z", "xl", "core"), ("y", "xh")
    placed = (P(None, col, row), P(col, row), P(row, col), P(row, col))
    return jax.shard_map(
        body, mesh=split, in_specs=placed, out_specs=P(None, col, row), check_vma=False
    )
```

```python
import jax
import jax.numpy as jnp
from jax import lax
from jax.sharding import Mesh, PartitionSpec as P

AXES = ("z", "xl", "core", "y", "xh")
HIGH = lax.Precision.HIGH


def index(z, x, core, y):
    return (((z * 2 + x % 2) * 2 + core) * 4 + y) * 2 + x // 2


def flip(value, per_core):
    pairs = []
    for z in range(4):
        for x in range(4):
            for core in range(2):
                for y in range(4):
                    if per_core == "core":
                        target = index(z, x, 1 - core, y)
                    else:
                        dz, dx, dy = per_core[core]
                        target = index(z ^ dz, x ^ dx, core, y ^ dy)
                    pairs.append((index(z, x, core, y), target))
    return lax.ppermute(value, AXES, pairs)


Z1, Z3, Y1, Y3 = (1, 0, 0), (3, 0, 0), (0, 0, 1), (0, 0, 3)
X1, X2, X3 = (0, 1, 0), (0, 2, 0), (0, 3, 0)
ZA, ZB, YA, YB, XL, XH = (Z1, Z3), (Z3, Z1), (Y1, Y3), (Y3, Y1), (X1, X1), (X2, X2)
XA, XB = (X1, X3), (X3, X1)
XN = (X3, X3)


def grow(value, step, axis):
    return jnp.concatenate([value, flip(value, step)], axis=axis)


def alternate(value, axis, size):
    blocks = [lax.slice_in_dim(value, i, i + size, axis=axis) for i in range(0, value.shape[axis], size)]
    return jnp.concatenate(blocks[::2], axis=axis), jnp.concatenate(blocks[1::2], axis=axis)


def trade(value, step, axis, size):
    kept, sent = alternate(value, axis, size)
    return kept + flip(sent, step)


def dot(spec, a, b):
    return jnp.einsum(spec, a, b, precision=HIGH, preferred_element_type=jnp.float32)


def in_parts(v):
    first = v[:, :, :, :32].transpose(1, 0, 2, 3, 4).reshape(256, -1)
    second = v[:, :, :, 32:].transpose(0, 2, 1, 3, 4).reshape(256, -1)
    return jnp.concatenate([first, second], axis=0)


def square(core, own, near):
    size = own.shape[0]
    got = flip(jnp.concatenate([own, near], axis=0), XB)
    far, both = got[:size], got[size:]
    first = core == 0
    top = jnp.concatenate([own, jnp.where(first, near, far)], axis=1)
    bottom = jnp.concatenate([both, jnp.where(first, far, near)], axis=1)
    return top, bottom


def body(trials, valence, conduction, screened):
    core = lax.axis_index("core")
    mine = lax.dynamic_index_in_dim(trials, core, 0, keepdims=False)
    theirs = lax.dynamic_index_in_dim(trials, 1 - core, 0, keepdims=False)

    c = grow(conduction, XL, 0)
    v = grow(valence, YA, 0)
    t = jnp.concatenate([mine, flip(theirs, "core")], axis=1)
    t = t.reshape(2, 32, 128)
    t = grow(t, ZA, 2)
    t, v = lax.optimization_barrier((t, v))
    v = grow(v, XH, 0)
    t = grow(t, ZB, 2)
    t, c = lax.optimization_barrier((t, c))
    c = grow(c, ZA, 0)
    p, q = t[0], t[1]
    q_near = flip(q, XA)
    p = grow(p, YA, 0)
    p, q, q_near, v, c = lax.optimization_barrier((p, q, q_near, v, c))
    c_near = flip(c, "core")
    c_far = flip(c, ZB)
    q = jnp.concatenate(square(core, q, q_near), axis=0)
    p = grow(p, YB, 0)
    p, q = lax.optimization_barrier((p, q))
    p_near = flip(p, XA)
    q = grow(q, YA, 0)
    p, p_near, q, c_near, c_far = lax.optimization_barrier((p, p_near, q, c_near, c_far))
    v = grow(v, YB, 0)
    c_other = jnp.concatenate([c_near, flip(c_far, "core")], axis=0)
    c = jnp.concatenate([c, c_far], axis=0)
    p = jnp.concatenate(square(core, p, p_near), axis=0)
    q = grow(q, YB, 0)
    p, v = lax.optimization_barrier((p, v))

    c_own = c.reshape(2, 2, 2, 64, 1024).transpose(2, 0, 1, 3, 4)
    c_other = c_other.reshape(2, 2, 2, 64, 1024).transpose(2, 1, 0, 3, 4)
    c_all = jnp.stack([c_own, c_other], axis=3).reshape(1024, 1024)
    v = v.reshape(2, 2, 2, 64, 512)
    v_mine, v_theirs = in_parts(v), in_parts(v.swapaxes(0, 2))

    half_p = dot("vc,cn->vn", p, c_all)
    got_p = flip(half_p, "core")
    half_q = dot("vc,cn->vn", q, c_all)
    got_q = flip(half_q, "core")
    half_mine = jnp.concatenate([half_p, half_q], axis=0)
    half_theirs = jnp.concatenate([got_p, got_q], axis=0)
    pairs_mine = screened * dot("vm,vn->mn", v_mine, half_mine)
    pairs_theirs = screened * dot("vm,vn->mn", v_theirs, half_theirs)
    to_p = flip(dot("vm,mn->vn", v_theirs[:256], pairs_theirs), "core")
    to_q = flip(dot("vm,mn->vn", v_theirs[256:], pairs_theirs), "core")
    sums_p = dot("vm,mn->vn", v_mine[:256], pairs_mine) + to_p
    sums_q = dot("vm,mn->vn", v_mine[256:], pairs_mine) + to_q
    p = dot("vn,cn->vc", sums_p, c_all)
    q = dot("vn,cn->vc", sums_q, c_all)
    p = trade(p, ZB, 1, 256)
    q = trade(q, YB, 0, 128)
    p = trade(p, YB, 0, 64)
    q = trade(q, ZB, 1, 256)
    p_kept, p_sent = alternate(p, 0, 32)
    q_kept, q_sent = alternate(q, 0, 64)
    r = jnp.concatenate([p_kept, q_kept], axis=0) + flip(jnp.concatenate([p_sent, q_sent], axis=0), YA)
    r = trade(r, ZA, 1, 128)
    kept, sent = alternate(r, 0, 32)
    r = kept + flip(jnp.concatenate([sent[:, 128:], sent[:, :128]], axis=1), XN)
    r = trade(r, XL, 1, 128)
    kept = r[:, :64]
    got = flip(r[:, 64:], "core")
    first = core == 0
    return jnp.stack([jnp.where(first, kept, got), jnp.where(first, got, kept)])


def solution(mesh):
    split = Mesh(mesh.devices.reshape(4, 2, 2, 4, 2), AXES)
    row, col = ("z", "xl", "core"), ("y", "xh")
    placed = (P(None, col, row), P(col, row), P(row, col), P(row, col))
    return jax.shard_map(
        body, mesh=split, in_specs=placed, out_specs=P(None, col, row), check_vma=False
    )
```

```python
import jax
import jax.numpy as jnp
from jax import lax
from jax.sharding import Mesh, PartitionSpec as P

AXES = ("z", "xl", "core", "y", "xh")
HIGH = lax.Precision.HIGH


def index(z, x, core, y):
    return (((z * 2 + x % 2) * 2 + core) * 4 + y) * 2 + x // 2


def flip(value, per_core):
    pairs = []
    for z in range(4):
        for x in range(4):
            for core in range(2):
                for y in range(4):
                    if per_core == "core":
                        target = index(z, x, 1 - core, y)
                    else:
                        dz, dx, dy = per_core[core]
                        target = index(z ^ dz, x ^ dx, core, y ^ dy)
                    pairs.append((index(z, x, core, y), target))
    return lax.ppermute(value, AXES, pairs)


Z1, Z3, Y1, Y3 = (1, 0, 0), (3, 0, 0), (0, 0, 1), (0, 0, 3)
X1, X2, X3 = (0, 1, 0), (0, 2, 0), (0, 3, 0)
ZA, ZB, YA, YB, XL, XH = (Z1, Z3), (Z3, Z1), (Y1, Y3), (Y3, Y1), (X1, X1), (X2, X2)
XA, XB = (X1, X3), (X3, X1)
XN = (X3, X3)


def grow(value, step, axis):
    return jnp.concatenate([value, flip(value, step)], axis=axis)


def alternate(value, axis, size):
    blocks = [lax.slice_in_dim(value, i, i + size, axis=axis) for i in range(0, value.shape[axis], size)]
    return jnp.concatenate(blocks[::2], axis=axis), jnp.concatenate(blocks[1::2], axis=axis)


def trade(value, step, axis, size):
    kept, sent = alternate(value, axis, size)
    return kept + flip(sent, step)


def dot(spec, a, b):
    return jnp.einsum(spec, a, b, precision=HIGH, preferred_element_type=jnp.float32)


def in_parts(v):
    first = v[:, :, :, :32].transpose(1, 0, 2, 3, 4).reshape(256, -1)
    second = v[:, :, :, 32:].transpose(0, 2, 1, 3, 4).reshape(256, -1)
    return jnp.concatenate([first, second], axis=0)


def square(core, own, near):
    size = own.shape[0]
    got = flip(jnp.concatenate([own, near], axis=0), XB)
    far, both = got[:size], got[size:]
    first = core == 0
    top = jnp.concatenate([own, jnp.where(first, near, far)], axis=1)
    bottom = jnp.concatenate([both, jnp.where(first, far, near)], axis=1)
    return top, bottom


def body(trials, valence, conduction, screened):
    core = lax.axis_index("core")
    mine = lax.dynamic_index_in_dim(trials, core, 0, keepdims=False)
    theirs = lax.dynamic_index_in_dim(trials, 1 - core, 0, keepdims=False)

    c = grow(conduction, XL, 0)
    v = grow(valence, YA, 0)
    t = jnp.concatenate([mine, flip(theirs, "core")], axis=1)
    t = t.reshape(2, 32, 128)
    t = grow(t, ZA, 2)
    t, v = lax.optimization_barrier((t, v))
    v = grow(v, XH, 0)
    t = grow(t, ZB, 2)
    t, c = lax.optimization_barrier((t, c))
    c = grow(c, ZA, 0)
    p, q = t[0], t[1]
    q_near = flip(q, XA)
    p = grow(p, YA, 0)
    p, q, q_near, v, c = lax.optimization_barrier((p, q, q_near, v, c))
    c_near = flip(c, "core")
    c_far = flip(c, ZB)
    q = jnp.concatenate(square(core, q, q_near), axis=0)
    p = grow(p, YB, 0)
    p, q = lax.optimization_barrier((p, q))
    p_near = flip(p, XA)
    q = grow(q, YA, 0)
    p, p_near, q, c_near, c_far = lax.optimization_barrier((p, p_near, q, c_near, c_far))
    v = grow(v, YB, 0)
    c_other = jnp.concatenate([c_near, flip(c_far, "core")], axis=0)
    c = jnp.concatenate([c, c_far], axis=0)
    p = jnp.concatenate(square(core, p, p_near), axis=0)
    q = grow(q, YB, 0)
    p, v = lax.optimization_barrier((p, v))

    c_own = c.reshape(2, 2, 2, 64, 1024).transpose(2, 0, 1, 3, 4)
    c_other = c_other.reshape(2, 2, 2, 64, 1024).transpose(2, 1, 0, 3, 4)
    c_all = jnp.stack([c_own, c_other], axis=3).reshape(1024, 1024)
    v = v.reshape(2, 2, 2, 64, 512)
    v_mine, v_theirs = in_parts(v), in_parts(v.swapaxes(0, 2))

    half_mine = dot("vc,cn->vn", jnp.concatenate([p, q], axis=0), c_all)
    half_theirs = flip(half_mine, "core")
    pairs_mine = screened * dot("vm,vn->mn", v_mine, half_mine)
    sums = dot("vm,mn->vn", v_mine, pairs_mine)
    sums, half_theirs = lax.optimization_barrier((sums, half_theirs))
    pairs_theirs = screened * dot("vm,vn->mn", v_theirs, half_theirs)
    to_p = flip(dot("vm,mn->vn", v_theirs[:256], pairs_theirs), "core")
    to_q = flip(dot("vm,mn->vn", v_theirs[256:], pairs_theirs), "core")
    p = dot("vn,cn->vc", sums[:256] + to_p, c_all)
    q = dot("vn,cn->vc", sums[256:] + to_q, c_all)
    p = trade(p, ZB, 1, 256)
    q = trade(q, YB, 0, 128)
    p = trade(p, YB, 0, 64)
    q = trade(q, ZB, 1, 256)
    p_kept, p_sent = alternate(p, 0, 32)
    q_kept, q_sent = alternate(q, 0, 64)
    r = jnp.concatenate([p_kept, q_kept], axis=0) + flip(jnp.concatenate([p_sent, q_sent], axis=0), YA)
    r = trade(r, ZA, 1, 128)
    kept, sent = alternate(r, 0, 32)
    r = kept + flip(jnp.concatenate([sent[:, 128:], sent[:, :128]], axis=1), XN)
    r = trade(r, XL, 1, 128)
    kept = r[:, :64]
    got = flip(r[:, 64:], "core")
    first = core == 0
    return jnp.stack([jnp.where(first, kept, got), jnp.where(first, got, kept)])


def solution(mesh):
    split = Mesh(mesh.devices.reshape(4, 2, 2, 4, 2), AXES)
    row, col = ("z", "xl", "core"), ("y", "xh")
    placed = (P(None, col, row), P(col, row), P(row, col), P(row, col))
    return jax.shard_map(
        body, mesh=split, in_specs=placed, out_specs=P(None, col, row), check_vma=False
    )
```

```python
import jax
import jax.numpy as jnp
from jax import lax
from jax.sharding import Mesh, PartitionSpec as P

AXES = ("z", "xl", "core", "y", "xh")
HIGH = lax.Precision.HIGH


def index(z, x, core, y):
    return (((z * 2 + x % 2) * 2 + core) * 4 + y) * 2 + x // 2


def flip(value, per_core):
    pairs = []
    for z in range(4):
        for x in range(4):
            for core in range(2):
                for y in range(4):
                    if per_core == "core":
                        target = index(z, x, 1 - core, y)
                    else:
                        dz, dx, dy = per_core[core]
                        target = index(z ^ dz, x ^ dx, core, y ^ dy)
                    pairs.append((index(z, x, core, y), target))
    return lax.ppermute(value, AXES, pairs)


Z1, Z3, Y1, Y3 = (1, 0, 0), (3, 0, 0), (0, 0, 1), (0, 0, 3)
X1, X2, X3 = (0, 1, 0), (0, 2, 0), (0, 3, 0)
ZA, ZB, YA, YB, XL, XH = (Z1, Z3), (Z3, Z1), (Y1, Y3), (Y3, Y1), (X1, X1), (X2, X2)
XA, XB = (X1, X3), (X3, X1)


def grow(value, step, axis):
    return jnp.concatenate([value, flip(value, step)], axis=axis)


def alternate(value, axis, size):
    blocks = [lax.slice_in_dim(value, i, i + size, axis=axis) for i in range(0, value.shape[axis], size)]
    return jnp.concatenate(blocks[::2], axis=axis), jnp.concatenate(blocks[1::2], axis=axis)


def trade(value, step, axis, size):
    kept, sent = alternate(value, axis, size)
    return kept + flip(sent, step)


def dot(spec, a, b):
    return jnp.einsum(spec, a, b, precision=HIGH, preferred_element_type=jnp.float32)


def in_parts(v):
    first = v[:, :, :, :32].transpose(1, 0, 2, 3, 4).reshape(256, -1)
    second = v[:, :, :, 32:].transpose(0, 2, 1, 3, 4).reshape(256, -1)
    return jnp.concatenate([first, second], axis=0)


def square(core, own, near):
    size = own.shape[0]
    got = flip(jnp.concatenate([own, near], axis=0), XB)
    far, both = got[:size], got[size:]
    first = core == 0
    top = jnp.concatenate([own, jnp.where(first, near, far)], axis=1)
    bottom = jnp.concatenate([both, jnp.where(first, far, near)], axis=1)
    return top, bottom


def body(trials, valence, conduction, screened):
    core = lax.axis_index("core")
    mine = lax.dynamic_index_in_dim(trials, core, 0, keepdims=False)
    theirs = lax.dynamic_index_in_dim(trials, 1 - core, 0, keepdims=False)

    c = grow(conduction, XL, 0)
    v = grow(valence, YA, 0)
    t = jnp.concatenate([mine, flip(theirs, "core")], axis=1)
    t = t.reshape(2, 32, 128)
    t = grow(t, ZA, 2)
    t, v = lax.optimization_barrier((t, v))
    v = grow(v, XH, 0)
    t = grow(t, ZB, 2)
    t, c = lax.optimization_barrier((t, c))
    c = grow(c, ZA, 0)
    p, q = t[0], t[1]
    q_near = flip(q, XA)
    p = grow(p, YA, 0)
    p, q, q_near, v, c = lax.optimization_barrier((p, q, q_near, v, c))
    c_near = flip(c, "core")
    c_far = flip(c, ZB)
    q = jnp.concatenate(square(core, q, q_near), axis=0)
    p = grow(p, YB, 0)
    p, q = lax.optimization_barrier((p, q))
    p_near = flip(p, XA)
    q = grow(q, YA, 0)
    p, p_near, q, c_near, c_far = lax.optimization_barrier((p, p_near, q, c_near, c_far))
    v = grow(v, YB, 0)
    c_other = jnp.concatenate([c_near, flip(c_far, "core")], axis=0)
    c = jnp.concatenate([c, c_far], axis=0)
    p = jnp.concatenate(square(core, p, p_near), axis=0)
    q = grow(q, YB, 0)
    p, v = lax.optimization_barrier((p, v))

    c_own = c.reshape(2, 2, 2, 64, 1024).transpose(2, 0, 1, 3, 4)
    c_other = c_other.reshape(2, 2, 2, 64, 1024).transpose(2, 1, 0, 3, 4)
    c_all = jnp.stack([c_own, c_other], axis=3).reshape(1024, 1024)
    v = v.reshape(2, 2, 2, 64, 512)
    v_mine, v_theirs = in_parts(v), in_parts(v.swapaxes(0, 2))

    half_mine = dot("vc,cn->vn", jnp.concatenate([p, q], axis=0), c_all)
    half_theirs = flip(half_mine, "core")
    pairs_mine = screened * dot("vm,vn->mn", v_mine, half_mine)
    sums = dot("vm,mn->vn", v_mine, pairs_mine)
    sums, half_theirs = lax.optimization_barrier((sums, half_theirs))
    pairs_theirs = screened * dot("vm,vn->mn", v_theirs, half_theirs)
    to_p = flip(dot("vm,mn->vn", v_theirs[:256], pairs_theirs), "core")
    to_q = flip(dot("vm,mn->vn", v_theirs[256:], pairs_theirs), "core")
    p = dot("vn,cn->vc", sums[:256] + to_p, c_all)
    q = dot("vn,cn->vc", sums[256:] + to_q, c_all)
    p = trade(p, ZB, 1, 256)
    q = trade(q, YB, 0, 128)
    p = trade(p, YB, 0, 64)
    q = trade(q, ZB, 1, 256)
    p_kept, p_sent = alternate(p, 0, 32)
    q_kept, q_sent = alternate(q, 0, 64)
    r = jnp.concatenate([p_kept, q_kept], axis=0) + flip(jnp.concatenate([p_sent, q_sent], axis=0), YA)
    r = trade(r, ZA, 1, 128)
    r = trade(r, XH, 0, 32)
    r = trade(r, XL, 1, 128)
    kept = r[:, :64]
    got = flip(r[:, 64:], "core")
    first = core == 0
    return jnp.stack([jnp.where(first, kept, got), jnp.where(first, got, kept)])


def solution(mesh):
    split = Mesh(mesh.devices.reshape(4, 2, 2, 4, 2), AXES)
    row, col = ("z", "xl", "core"), ("y", "xh")
    placed = (P(None, col, row), P(col, row), P(row, col), P(row, col))
    return jax.shard_map(
        body, mesh=split, in_specs=placed, out_specs=P(None, col, row), check_vma=False
    )
```
